32 devices in a mesh: rep: 8 (over z, y), fsdp: 4 (over x, core).
Axes of the slice: x: 2, y: 2, z: 4, core: 2. Of those that a mesh axis runs over, the one named last changes fastest.
Arguments:
- weights: bfloat16 [8, 4, 1024, 512], P('rep', None, 'fsdp'), may hold values from -6 to 6
- momentum: bfloat16 [8, 4, 1024, 512], P('rep', None, 'fsdp')
- gradient: bfloat16 [8, 4, 1024, 512], P('rep', None, 'fsdp')
- partner: int32 [8], replicated, may hold values from 0 to 7, as said below
Outputs:
- averaged: bfloat16 [8, 4, 1024, 512], P('rep', None, 'fsdp')
The draws below stay inside these ranges and needn't reach their ends.
Inputs may be any that keep to these rules, and one draw needn't show every extreme that they name: partner[partner[r]] = r for every replica r, and partner[r] differs from r in exactly one bit of its binary index.
All inputs are finite; a program needn't handle non-finite values.
Results may differ from the reference program's by a relative error of at most 0.014.
Values may be sent and summed in bfloat16 or wider, within the bound.
A program may use at most 64 MiB of HBM per device.

```python
import math
import jax
import jax.numpy as jnp
from jax import lax

ROWS = 1024
COLS = 512
ITERS = 5
MATS = 4
REPLICAS = 8


def shared_scales(key):
    row_key, col_key = jax.random.split(key)
    row_scale = jnp.exp(jax.random.uniform(row_key, (REPLICAS, MATS, ROWS, 1), jnp.float32, jnp.log(0.3), jnp.log(3.0)))
    col_scale = jnp.exp(jax.random.uniform(col_key, (REPLICAS, MATS, 1, COLS), jnp.float32, jnp.log(0.3), jnp.log(3.0)))
    return row_scale * col_scale


def draw_momentum(key, part):
    scales = shared_scales(key)
    key = jax.random.fold_in(key, 11)
    full_shape = (REPLICAS, MATS, ROWS, COLS)
    values = jax.random.normal(key, full_shape, jnp.float32)
    return (values * scales).astype(jnp.bfloat16)


def draw_gradient(key, part):
    scales = shared_scales(key)
    key = jax.random.fold_in(key, 17)
    full_shape = (REPLICAS, MATS, ROWS, COLS)
    values = jax.random.normal(key, full_shape, jnp.float32)
    return (values * scales).astype(jnp.bfloat16)


def draw_partner(key, part):
    key = jax.random.fold_in(key, 29)
    bit_count = REPLICAS.bit_length() - 1
    index_row = jnp.arange(REPLICAS, dtype=jnp.int32)
    bit_row = jnp.arange(bit_count, dtype=jnp.int32)
    used = jnp.zeros((REPLICAS, bit_count), jnp.int32)
    chosen = jnp.full((REPLICAS,), -1, jnp.int32)
    group_index = jnp.zeros((REPLICAS,), jnp.int32)
    for level in range(bit_count):
        ranks = jax.random.randint(jax.random.fold_in(key, 1000 + level), (2 ** level,), 0, bit_count - level)
        pick_rank = ranks[group_index]
        unused = 1 - used
        counted = jnp.cumsum(unused, axis=1)
        hit = (unused == 1) & (counted == pick_rank[:, None] + 1)
        bit_number = jnp.sum(jnp.where(hit, bit_row[None, :], 0), axis=1).astype(jnp.int32)
        coins = jax.random.randint(jax.random.fold_in(key, level), (2 ** level,), 0, 4)
        if level < bit_count - 1:
            picked = coins[group_index] == 0
        else:
            picked = index_row >= 0
        chosen = jnp.where((chosen < 0) & picked, bit_number, chosen)
        used = jnp.where(bit_row[None, :] == bit_number[:, None], 1, used)
        group_index = group_index * 2 + jnp.bitwise_and(jnp.right_shift(index_row, bit_number), 1)
    return jnp.bitwise_xor(index_row, jnp.left_shift(jnp.int32(1), chosen)).astype(jnp.int32)


def level_of(rng, shape, pieces, least, top_value):
    level, own = 1.0, jax.random.fold_in(rng, 6)
    for dim, blocks in pieces:
        steps = jnp.exp(jax.random.uniform(jax.random.fold_in(own, dim), (blocks,), jnp.float32, least / len(pieces), top_value / len(pieces)))
        level = level * jnp.repeat(steps, shape[dim] // blocks).reshape([-1 if axis == dim else 1 for axis in range(len(shape))])
    return level


def centred(own_key, dims, width, most, cuts=(), kind=jnp.bfloat16):
    result = jax.random.normal(own_key, dims, jnp.float32) * width
    if len(cuts) > 0:
        result = level_of(own_key, dims, cuts, -0.22, 0.18) * result
    return jnp.clip(result, min=-most, max=most).astype(kind)


def setup_inputs(seed: int = 0) -> dict:
    splits = jax.random.split(jax.random.key(seed), 5)
    weights = centred(splits[0], (REPLICAS, MATS, ROWS, COLS), 1.0, 6.0, ((0, 8), (2, 4)))
    momentum = draw_momentum(jax.random.fold_in(splits[4], 71), 0)
    gradient = draw_gradient(jax.random.fold_in(splits[4], 71), 0)
    partner = draw_partner(jax.random.fold_in(splits[4], 71), 0)
    return dict(weights=weights, momentum=momentum, gradient=gradient, partner=partner)


beta_moment = 0.95
epsilon_norm = 1e-07
coef_first = 3.4445
coef_second = -4.775
coef_third = 2.0315
learn_rate = 1.0
decay_rate = 0.1

def newton_schulz(matrix):
    current = matrix.T
    for step in range(ITERS):
        gram = jnp.dot(current, current.T, preferred_element_type=jnp.float32)
        gram_low = gram.astype(jnp.bfloat16)
        square = jnp.dot(gram_low, gram_low, preferred_element_type=jnp.float32)
        poly = (coef_second * gram + coef_third * square).astype(jnp.bfloat16)
        current = (coef_first * current.astype(jnp.float32) + jnp.dot(poly, current, preferred_element_type=jnp.float32)).astype(jnp.bfloat16)
    return current.T

def reference(weights, momentum, gradient, partner):
    moment_new = (beta_moment * momentum.astype(jnp.float32) + gradient.astype(jnp.float32)).astype(jnp.bfloat16)
    wide = moment_new.astype(jnp.float32)
    total = lax.optimization_barrier(jnp.sum(wide * wide, axis=(2, 3), keepdims=True))
    start = (wide / (jnp.sqrt(total) + epsilon_norm)).astype(jnp.bfloat16)
    flat = start.reshape(REPLICAS * MATS, ROWS, COLS)
    update = lax.map(newton_schulz, flat).reshape(REPLICAS, MATS, ROWS, COLS)
    scale = learn_rate * 0.2 * math.sqrt(ROWS)
    stepped = (weights.astype(jnp.float32) * (1.0 - learn_rate * decay_rate) - scale * update.astype(jnp.float32)).astype(jnp.bfloat16)
    mates = jnp.take(stepped, partner, axis=0)
    return ((stepped.astype(jnp.float32) + mates.astype(jnp.float32)) * 0.5).astype(jnp.bfloat16)
```

```python
import functools
import math

import jax
import jax.numpy as jnp
from jax import lax
from jax.experimental import pallas as pl
from jax.experimental.pallas import tpu as pltpu
from jax.sharding import PartitionSpec as P

ITERS = 5

beta_moment = 0.95
epsilon_norm = 1e-07
coef_first = 3.4445
coef_second = -4.775
coef_third = 2.0315
learn_rate = 1.0
decay_rate = 0.1

MESH = pl.DeviceIdType.MESH
BF16, F32 = jnp.bfloat16, jnp.float32


def swapped(value, axis, distance):
    mask = 2**distance
    pairs = [(source, source ^ mask) for source in range(lax.axis_size(axis))]
    return lax.ppermute(value, axis, pairs)


def flipped(index, mask):
    result = index
    bit = 1
    while bit <= mask:
        if mask & bit:
            result = result + bit * (1 - 2 * (lax.div(index, bit) % 2))
        bit *= 2
    return result


def kernel(count, masks, w_hbm, m_hbm, g_hbm, out_hbm, w_v, m_v, g_v, stage, arrived, x, gram, gram_low, poly,
           update_out, update_in, stepped, received, averaged, load_sem, store_sem, send_sem, recv_sem):
    rep, me = lax.axis_index("rep"), lax.axis_index("fsdp")
    rows = w_v.shape[1]
    cols = w_v.shape[2]
    row_count = rows * count
    block = rows if rows % 128 == 0 else 256
    peer = [flipped(me, d) for d in range(count)]
    order = list(range(count - 1, -1, -1))

    loads = {}
    for d in order:
        loads[d] = [
            pltpu.make_async_copy(m_hbm.at[peer[d]], m_v.at[peer[d]], load_sem.at[0, d]),
            pltpu.make_async_copy(g_hbm.at[peer[d]], g_v.at[peer[d]], load_sem.at[1, d]),
        ]
        for copy in loads[d]:
            copy.start()
    weight_loads = [pltpu.make_async_copy(w_hbm.at[peer[d]], w_v.at[peer[d]], load_sem.at[2, d]) for d in range(count)]
    for copy in weight_loads:
        copy.start()

    barrier = pltpu.get_barrier_semaphore()
    for d in range(1, count):
        pl.semaphore_signal(barrier, inc=1, device_id=(rep, peer[d]), device_id_type=MESH)
    greeted = count - 1
    if masks is not None:
        first, last = masks
        if first == last:
            mate = flipped(rep, first)
        else:
            side = lax.div(rep, 7 - first - last) % 2
            mate = flipped(rep, first) * (1 - side) + flipped(rep, last) * side
        pl.semaphore_signal(barrier, inc=1, device_id=(mate, me), device_id_type=MESH)
        greeted += 1

    def to_peer(kind, d, source, target):
        return pltpu.make_async_remote_copy(
            src_ref=source, dst_ref=target, send_sem=send_sem.at[kind, d], recv_sem=recv_sem.at[kind, d],
            device_id=(rep, peer[d]), device_id_type=MESH)

    sent = []
    for d in order:
        for copy in loads[d]:
            copy.wait()
        blended = beta_moment * m_v[peer[d]].astype(F32) + g_v[peer[d]].astype(F32)
        if d == order[0]:
            pl.semaphore_wait(barrier, greeted)
        if d:
            stage[d] = blended.astype(BF16)
            copy = to_peer(0, d, stage.at[d], arrived.at[me])
            copy.start()
            sent.append(copy)
        else:
            arrived[me] = blended.astype(BF16)

    total = jnp.zeros((1, 1), F32)
    by_block = block == rows
    for d in range(count):
        if d:
            sent[count - 1 - d].wait_recv()
        wide = arrived[peer[d]].astype(F32)
        total = total + jnp.sum(wide * wide, axis=(0, 1), keepdims=True)
        if by_block:
            place = pl.ds(pl.multiple_of(peer[d] * rows, rows), rows)
            x[:, place] = jnp.swapaxes(arrived[peer[d]], 0, 1)
    if not by_block:
        whole = arrived[...].reshape(row_count, cols)
        for start in range(0, row_count, block):
            x[:, start : start + block] = jnp.swapaxes(whole[start : start + block], 0, 1)
    inverse = 1.0 / (jnp.sqrt(total) + epsilon_norm)
    x[...] = (x[...].astype(F32) * inverse).astype(BF16)

    half = cols // 2

    def make_poly():
        for top in (0, half):
            part = lax.dot_general(x[top : top + half, :], x[...], (((1,), (1,)), ((), ())), preferred_element_type=F32)
            gram[top : top + half, :] = part
            gram_low[top : top + half, :] = part.astype(BF16)
        for top in (0, half):
            square = jnp.dot(gram_low[top : top + half, :], gram_low[...], preferred_element_type=F32)
            poly[top : top + half, :] = (coef_second * gram[top : top + half, :] + coef_third * square).astype(BF16)

    def next_block(place):
        old = x[:, place]
        product = jnp.dot(poly[...], old, preferred_element_type=F32)
        return (coef_first * old.astype(F32) + product).astype(BF16)

    @pl.loop(0, ITERS - 1)
    def _(step):
        make_poly()
        for start in range(0, row_count, 256):
            place = slice(start, start + 256)
            x[:, place] = next_block(place)

    make_poly()
    returns = [None] * count
    if not by_block:
        for start in range(0, row_count, block):
            piece = jnp.swapaxes(next_block(slice(start, start + block)), 0, 1)
            many = block // rows
            update_out[start // rows : start // rows + many] = piece.reshape(many, rows, cols)
    for d in order:
        if by_block:
            place = pl.ds(pl.multiple_of(peer[d] * rows, rows), rows)
            update_out[peer[d]] = jnp.swapaxes(next_block(place), 0, 1)
        if d:
            returns[d] = to_peer(1, d, update_out.at[peer[d]], update_in.at[me])
            returns[d].start()

    scale = learn_rate * 0.2 * math.sqrt(row_count)
    passed, stores = [], []
    for d in range(count):
        weight_loads[d].wait()
        if d:
            returns[d].wait_recv()
            update = update_in[peer[d]]
        else:
            update = update_out[me]
        stepped[peer[d]] = (
            w_v[peer[d]].astype(F32) * (1.0 - learn_rate * decay_rate) - scale * update.astype(F32)
        ).astype(BF16)
        if masks is not None:
            copy = pltpu.make_async_remote_copy(
                src_ref=stepped.at[peer[d]], dst_ref=received.at[peer[d]], send_sem=send_sem.at[2, d],
                recv_sem=recv_sem.at[2, d], device_id=(mate, me), device_id_type=MESH)
            copy.start()
            passed.append(copy)
        else:
            copy = pltpu.make_async_copy(stepped.at[peer[d]], out_hbm.at[peer[d]], store_sem.at[d])
            copy.start()
            stores.append(copy)
    for d, copy in enumerate(passed):
        copy.wait_recv()
        averaged[peer[d]] = ((stepped[peer[d]].astype(F32) + received[peer[d]].astype(F32)) * 0.5).astype(BF16)
        store = pltpu.make_async_copy(averaged.at[peer[d]], out_hbm.at[peer[d]], store_sem.at[d])
        store.start()
        stores.append(store)
    for copy in sent + returns[1:] + passed:
        copy.wait_send()
    for copy in stores:
        copy.wait()


def step_call(masks, number, weights, momentum, gradient):
    count = lax.axis_size("fsdp")
    _, mats, rows, cols = weights.shape
    tile = pltpu.VMEM((count, rows, cols), BF16)
    row_count = rows * count
    result = pl.pallas_call(
        functools.partial(kernel, count, masks),
        out_shape=jax.ShapeDtypeStruct((mats, rows, cols), BF16),
        in_specs=[pl.BlockSpec(memory_space=pl.ANY)] * 3,
        out_specs=pl.BlockSpec(memory_space=pl.ANY),
        scratch_shapes=[tile] * 5
        + [
            pltpu.VMEM((cols, row_count), BF16),
            pltpu.VMEM((cols, cols), F32),
            pltpu.VMEM((cols, cols), BF16),
            pltpu.VMEM((cols, cols), BF16),
        ]
        + [tile] * 5
        + [
            pltpu.SemaphoreType.DMA((3, count)),
            pltpu.SemaphoreType.DMA((count,)),
            pltpu.SemaphoreType.DMA((3, count)),
            pltpu.SemaphoreType.DMA((3, count)),
        ],
        compiler_params=pltpu.CompilerParams(
            collective_id=number, has_side_effects=True, vmem_limit_bytes=40 * 1024 * 1024
        ),
    )(weights[0], momentum[0], gradient[0])
    return result[None]


def averaged_by_permutes(stepped, partner):
    rep_count = lax.axis_size("rep")
    own_index = lax.axis_index("rep")
    differ = jnp.bitwise_xor(partner[own_index], own_index)
    received = jnp.zeros_like(stepped)
    for bit_number in range(rep_count.bit_length() - 1):
        other = swapped(stepped, "rep", bit_number)
        received = jnp.where(differ == 1 << bit_number, other, received)
    return ((stepped.astype(F32) + received.astype(F32)) * 0.5).astype(BF16)


def local(weights, momentum, gradient, partner):
    if lax.axis_size("rep") != 8:
        return averaged_by_permutes(step_call(None, 0, weights, momentum, gradient), partner)
    case = 3 * (partner[0] // 2) + jnp.bitwise_xor(partner[7], 7) // 2
    branches = [
        functools.partial(step_call, (first, last), 3 * row + column)
        for row, first in enumerate((1, 2, 4))
        for column, last in enumerate((1, 2, 4))
    ]
    return lax.switch(case, branches, weights, momentum, gradient)


def solution(mesh):
    spec = P("rep", None, "fsdp", None)
    return jax.shard_map(local, mesh=mesh, in_specs=(spec, spec, spec, P()), out_specs=spec, check_vma=False)
```

```python
import functools
import math

import jax
import jax.numpy as jnp
from jax import lax
from jax.experimental import pallas as pl
from jax.experimental.pallas import tpu as pltpu
from jax.sharding import PartitionSpec as P

ITERS = 5

beta_moment = 0.95
epsilon_norm = 1e-07
coef_first = 3.4445
coef_second = -4.775
coef_third = 2.0315
learn_rate = 1.0
decay_rate = 0.1

MESH = pl.DeviceIdType.MESH
BF16, F32 = jnp.bfloat16, jnp.float32


def swapped(value, axis, distance):
    mask = 2**distance
    pairs = [(source, source ^ mask) for source in range(lax.axis_size(axis))]
    return lax.ppermute(value, axis, pairs)


def flipped(index, mask):
    result = index
    bit = 1
    while bit <= mask:
        if mask & bit:
            result = result + bit * (1 - 2 * (lax.div(index, bit) % 2))
        bit *= 2
    return result


def greet(devices):
    barrier = pltpu.get_barrier_semaphore()
    for device in devices:
        pl.semaphore_signal(barrier, inc=1, device_id=device, device_id_type=MESH)


def greeted(number):
    pl.semaphore_wait(pltpu.get_barrier_semaphore(), number)


def gather_and_iterate(count, m_hbm, g_hbm, partner_hbm, update, case, m_v, g_v, stage, arrived, x, gram, gram_low, poly,
                       partner, partner_sem, load_sem, send_sem, recv_sem):
    rep, me = lax.axis_index("rep"), lax.axis_index("fsdp")
    rows, cols = m_v.shape[1:]
    row_count = rows * count
    block = rows if rows % 128 == 0 else 256
    by_block = block == rows
    peer = [flipped(me, d) for d in range(count)]
    order = list(range(count - 1, -1, -1))

    loads = {}
    for d in order:
        loads[d] = [
            pltpu.make_async_copy(m_hbm.at[peer[d]], m_v.at[peer[d]], load_sem.at[0, d]),
            pltpu.make_async_copy(g_hbm.at[peer[d]], g_v.at[peer[d]], load_sem.at[1, d]),
        ]
        for copy in loads[d]:
            copy.start()
    partner_load = pltpu.make_async_copy(partner_hbm, partner, partner_sem)
    partner_load.start()
    greet([(rep, peer[d]) for d in range(1, count)])

    sent = {}
    for d in order:
        for copy in loads[d]:
            copy.wait()
        blended = beta_moment * m_v[peer[d]].astype(F32) + g_v[peer[d]].astype(F32)
        if d == order[0]:
            greeted(count - 1)
        if d:
            stage[d] = blended.astype(BF16)
            sent[d] = pltpu.make_async_remote_copy(
                src_ref=stage.at[d], dst_ref=arrived.at[me], send_sem=send_sem.at[d], recv_sem=recv_sem.at[d],
                device_id=(rep, peer[d]), device_id_type=MESH)
            sent[d].start()
        else:
            arrived[me] = blended.astype(BF16)

    partner_load.wait()
    last = partner_hbm.shape[0] - 1
    case[0] = 3 * lax.div(partner[0], 2) + lax.div(last - partner[last], 2)

    total = jnp.zeros((1, 1), F32)
    for d in range(count):
        if d:
            sent[d].wait_recv()
        wide = arrived[peer[d]].astype(F32)
        total = total + jnp.sum(wide * wide, axis=(0, 1), keepdims=True)
        if by_block:
            place = pl.ds(pl.multiple_of(peer[d] * rows, rows), rows)
            x[:, place] = jnp.swapaxes(arrived[peer[d]], 0, 1)
    if not by_block:
        whole = arrived[...].reshape(row_count, cols)
        for start in range(0, row_count, block):
            x[:, start : start + block] = jnp.swapaxes(whole[start : start + block], 0, 1)
    inverse = 1.0 / (jnp.sqrt(total) + epsilon_norm)
    x[...] = (x[...].astype(F32) * inverse).astype(BF16)

    half = cols // 2

    def make_poly():
        for top in (0, half):
            part = lax.dot_general(x[top : top + half, :], x[...], (((1,), (1,)), ((), ())), preferred_element_type=F32)
            gram[top : top + half, :] = part
            gram_low[top : top + half, :] = part.astype(BF16)
        for top in (0, half):
            square = jnp.dot(gram_low[top : top + half, :], gram_low[...], preferred_element_type=F32)
            poly[top : top + half, :] = (coef_second * gram[top : top + half, :] + coef_third * square).astype(BF16)

    def next_block(place):
        old = x[:, place]
        product = jnp.dot(poly[...], old, preferred_element_type=F32)
        return (coef_first * old.astype(F32) + product).astype(BF16)

    @pl.loop(0, ITERS - 1)
    def _(step):
        make_poly()
        for start in range(0, row_count, 256):
            place = slice(start, start + 256)
            x[:, place] = next_block(place)

    make_poly()
    for start in range(0, row_count, block):
        piece = jnp.swapaxes(next_block(slice(start, start + block)), 0, 1)
        update[start // rows : (start + block) // rows] = piece.reshape(block // rows, rows, cols)
    for d in range(1, count):
        sent[d].wait_send()


def return_and_average(count, masks, update, w_hbm, averaged, w_v, update_in, stepped, received, load_sem, send_sem,
                       recv_sem):
    rep, me = lax.axis_index("rep"), lax.axis_index("fsdp")
    rows = w_v.shape[1]
    peer = [flipped(me, d) for d in range(count)]
    loads = [pltpu.make_async_copy(w_hbm.at[peer[d]], w_v.at[peer[d]], load_sem.at[d]) for d in range(count)]
    for copy in loads:
        copy.start()
    known = [(rep, peer[d]) for d in range(1, count)]
    if masks is not None:
        first, last = masks
        if first == last:
            mate = flipped(rep, first)
        else:
            side = lax.div(rep, 7 - first - last) % 2
            mate = flipped(rep, first) * (1 - side) + flipped(rep, last) * side
        known.append((mate, me))
    greet(known)
    greeted(len(known))

    returns = {}
    for d in range(count - 1, 0, -1):
        returns[d] = pltpu.make_async_remote_copy(
            src_ref=update.at[peer[d]], dst_ref=update_in.at[me], send_sem=send_sem.at[0, d],
            recv_sem=recv_sem.at[0, d], device_id=(rep, peer[d]), device_id_type=MESH)
        returns[d].start()

    scale = learn_rate * 0.2 * math.sqrt(rows * count)
    passed = []
    for d in range(count):
        loads[d].wait()
        if d:
            returns[d].wait_recv()
            part = update_in[peer[d]]
        else:
            part = update[me]
        stepped[peer[d]] = (
            w_v[peer[d]].astype(F32) * (1.0 - learn_rate * decay_rate) - scale * part.astype(F32)
        ).astype(BF16)
        if masks is not None:
            copy = pltpu.make_async_remote_copy(
                src_ref=stepped.at[peer[d]], dst_ref=received.at[peer[d]], send_sem=send_sem.at[1, d],
                recv_sem=recv_sem.at[1, d], device_id=(mate, me), device_id_type=MESH)
            copy.start()
            passed.append(copy)
    if masks is None:
        averaged[...] = stepped[...]
    for d, copy in enumerate(passed):
        copy.wait_recv()
        averaged[peer[d]] = ((stepped[peer[d]].astype(F32) + received[peer[d]].astype(F32)) * 0.5).astype(BF16)
    for copy in list(returns.values()) + passed:
        copy.wait_send()


def params(number, limit):
    return pltpu.CompilerParams(collective_id=number, has_side_effects=True, vmem_limit_bytes=limit * 1024 * 1024)


def orthogonalized(number, momentum, gradient, partner):
    count = lax.axis_size("fsdp")
    _, _, rows, cols = momentum.shape
    tile = pltpu.VMEM((count, rows, cols), BF16)
    square = (cols, cols)
    return pl.pallas_call(
        functools.partial(gather_and_iterate, count),
        out_shape=[jax.ShapeDtypeStruct((count, rows, cols), BF16), jax.ShapeDtypeStruct((1,), jnp.int32)],
        in_specs=[pl.BlockSpec(memory_space=pltpu.HBM)] * 3,
        out_specs=[pl.BlockSpec(memory_space=pltpu.VMEM), pl.BlockSpec(memory_space=pltpu.SMEM)],
        scratch_shapes=[tile] * 4
        + [pltpu.VMEM((cols, rows * count), BF16), pltpu.VMEM(square, F32)]
        + [pltpu.VMEM(square, BF16)] * 2
        + [pltpu.SMEM(partner.shape, jnp.int32), pltpu.SemaphoreType.DMA]
        + [pltpu.SemaphoreType.DMA((2, count)), pltpu.SemaphoreType.DMA((count,)), pltpu.SemaphoreType.DMA((count,))],
        compiler_params=params(number, 60),
    )(momentum[0], gradient[0], partner)


def finished(masks, number, update, weights):
    count = lax.axis_size("fsdp")
    tile = pltpu.VMEM(weights.shape[1:], BF16)
    return pl.pallas_call(
        functools.partial(return_and_average, count, masks),
        out_shape=jax.ShapeDtypeStruct(weights.shape[1:], BF16),
        in_specs=[pl.BlockSpec(memory_space=pltpu.VMEM), pl.BlockSpec(memory_space=pltpu.HBM)],
        out_specs=pl.BlockSpec(memory_space=pltpu.VMEM),
        scratch_shapes=[tile] * 4
        + [pltpu.SemaphoreType.DMA((count,))]
        + [pltpu.SemaphoreType.DMA((2, count))] * 2,
        compiler_params=params(number, 24),
    )(update, weights[0])


def averaged_by_permutes(stepped, partner):
    rep_count = lax.axis_size("rep")
    own_index = lax.axis_index("rep")
    differ = jnp.bitwise_xor(partner[own_index], own_index)
    received = jnp.zeros_like(stepped)
    for bit_number in range(rep_count.bit_length() - 1):
        other = swapped(stepped, "rep", bit_number)
        received = jnp.where(differ == 1 << bit_number, other, received)
    return ((stepped.astype(F32) + received.astype(F32)) * 0.5).astype(BF16)


def local(weights, momentum, gradient, partner):
    update, case = orthogonalized(0, momentum, gradient, partner)
    if lax.axis_size("rep") != 8:
        return averaged_by_permutes(finished(None, 1, update, weights)[None], partner)
    branches = [
        functools.partial(finished, (first, last), 1 + 3 * row + column)
        for row, first in enumerate((1, 2, 4))
        for column, last in enumerate((1, 2, 4))
    ]
    return lax.switch(case[0], branches, update, weights)[None]


def solution(mesh):
    spec = P("rep", None, "fsdp", None)
    return jax.shard_map(local, mesh=mesh, in_specs=(spec, spec, spec, P()), out_specs=spec, check_vma=False)
```

```python
import functools
import math

import jax
import jax.numpy as jnp
from jax import lax
from jax.experimental import pallas as pl
from jax.experimental.pallas import tpu as pltpu
from jax.sharding import PartitionSpec as P

ITERS = 5

beta_moment = 0.95
epsilon_norm = 1e-07
coef_first = 3.4445
coef_second = -4.775
coef_third = 2.0315
learn_rate = 1.0
decay_rate = 0.1

MESH = pl.DeviceIdType.MESH
BF16, F32 = jnp.bfloat16, jnp.float32


def swapped(value, axis, distance):
    mask = 2**distance
    pairs = [(source, source ^ mask) for source in range(lax.axis_size(axis))]
    return lax.ppermute(value, axis, pairs)


def flipped(index, mask):
    result = index
    bit = 1
    while bit <= mask:
        if mask & bit:
            result = result + bit * (1 - 2 * (lax.div(index, bit) % 2))
        bit *= 2
    return result


PIECES = 2


def pieces(rows):
    length = rows // PIECES if rows % (PIECES * 128) == 0 else rows
    return [pl.ds(start, length) for start in range(0, rows, length)]


def greet(devices):
    barrier = pltpu.get_barrier_semaphore()
    for device in devices:
        pl.semaphore_signal(barrier, inc=1, device_id=device, device_id_type=MESH)


def greeted(number):
    pl.semaphore_wait(pltpu.get_barrier_semaphore(), number)


def gather_and_iterate(count, m_hbm, g_hbm, partner_hbm, update, case, m_v, g_v, stage, arrived, x, gram, gram_low, poly,
                       partner, partner_sem, load_sem, send_sem, recv_sem):
    rep, me = lax.axis_index("rep"), lax.axis_index("fsdp")
    rows, cols = m_v.shape[1:]
    row_count = rows * count
    block = rows if rows % 128 == 0 else 256
    by_block = block == rows
    peer = [flipped(me, d) for d in range(count)]
    order = list(range(count - 1, -1, -1))

    parts = pieces(rows)
    loads = {}
    for d in order:
        for number, part in enumerate(parts):
            loads[d, number] = [
                pltpu.make_async_copy(m_hbm.at[peer[d], part], m_v.at[peer[d], part], load_sem.at[0, d, number]),
                pltpu.make_async_copy(g_hbm.at[peer[d], part], g_v.at[peer[d], part], load_sem.at[1, d, number]),
            ]
            for copy in loads[d, number]:
                copy.start()
    partner_load = pltpu.make_async_copy(partner_hbm, partner, partner_sem)
    partner_load.start()
    greet([(rep, peer[d]) for d in range(1, count)])

    sent = {}
    for d in order:
        for number, part in enumerate(parts):
            for copy in loads[d, number]:
                copy.wait()
            blended = beta_moment * m_v[peer[d], part].astype(F32) + g_v[peer[d], part].astype(F32)
            if d:
                stage[d, part] = blended.astype(BF16)
                if d == order[0] and number == 0:
                    greeted(count - 1)
                sent[d, number] = pltpu.make_async_remote_copy(
                    src_ref=stage.at[d, part], dst_ref=arrived.at[me, part], send_sem=send_sem.at[d, number],
                    recv_sem=recv_sem.at[d, number], device_id=(rep, peer[d]), device_id_type=MESH)
                sent[d, number].start()
            else:
                arrived[me, part] = blended.astype(BF16)

    partner_load.wait()
    last = partner_hbm.shape[0] - 1
    case[0] = 3 * lax.div(partner[0], 2) + lax.div(last - partner[last], 2)

    total = jnp.zeros((1, 1), F32)
    for d in [0, 1] + list(range(count - 1, 1, -1)):
        for number, part in enumerate(parts):
            if d:
                sent[d, number].wait_recv()
            wide = arrived[peer[d], part].astype(F32)
            total = total + jnp.sum(wide * wide, axis=(0, 1), keepdims=True)
            if by_block:
                place = pl.ds(pl.multiple_of(peer[d] * rows + part.start, part.size), part.size)
                x[:, place] = jnp.swapaxes(arrived[peer[d], part], 0, 1)
    if not by_block:
        whole = arrived[...].reshape(row_count, cols)
        for start in range(0, row_count, block):
            x[:, start : start + block] = jnp.swapaxes(whole[start : start + block], 0, 1)
    inverse = 1.0 / (jnp.sqrt(total) + epsilon_norm)
    x[...] = (x[...].astype(F32) * inverse).astype(BF16)

    half = cols // 2

    def make_poly():
        left, right = slice(0, half), slice(half, cols)

        def outer(first, second):
            return lax.dot_general(
                x[first, :], x[second, :], (((1,), (1,)), ((), ())), preferred_element_type=F32
            )

        for first, second in ((left, left), (left, right), (right, right)):
            part = outer(first, second)
            gram[first, second] = part
            gram_low[first, second] = part.astype(BF16)
            if first != second:
                gram_low[second, first] = jnp.swapaxes(part.astype(BF16), 0, 1)
        for first, second in ((left, left), (left, right), (right, right)):
            square = jnp.dot(gram_low[first, :], gram_low[:, second], preferred_element_type=F32)
            part = (coef_second * gram[first, second] + coef_third * square).astype(BF16)
            poly[first, second] = part
            if first != second:
                poly[second, first] = jnp.swapaxes(part, 0, 1)

    def next_block(place):
        old = x[:, place]
        product = jnp.dot(poly[...], old, preferred_element_type=F32)
        return (coef_first * old.astype(F32) + product).astype(BF16)

    for step in range(ITERS - 1):
        make_poly()
        for start in range(0, row_count, 256):
            place = slice(start, start + 256)
            x[:, place] = next_block(place)

    make_poly()
    for start in range(0, row_count, block):
        piece = jnp.swapaxes(next_block(slice(start, start + block)), 0, 1)
        update[start // rows : (start + block) // rows] = piece.reshape(block // rows, rows, cols)
    for copy in sent.values():
        copy.wait_send()


def return_and_average(count, masks, update, w_hbm, averaged, w_v, update_in, stepped, received, load_sem, send_sem,
                       recv_sem):
    rep, me = lax.axis_index("rep"), lax.axis_index("fsdp")
    rows = w_v.shape[1]
    peer = [flipped(me, d) for d in range(count)]
    taken = [0, 1] + list(range(count - 1, 1, -1))
    parts = [pl.ds(0, rows)]
    every = [(d, number, part) for d in taken for number, part in enumerate(parts)]
    loads = {}
    for d, number, part in every:
        loads[d, number] = pltpu.make_async_copy(
            w_hbm.at[peer[d], part], w_v.at[peer[d], part], load_sem.at[d, number]
        )
        loads[d, number].start()
    known = [(rep, peer[d]) for d in range(1, count)]
    if masks is not None:
        first, last = masks
        if first == last:
            mate = flipped(rep, first)
        else:
            side = lax.div(rep, 7 - first - last) % 2
            mate = flipped(rep, first) * (1 - side) + flipped(rep, last) * side
        known.append((mate, me))
    greet(known)
    greeted(len(known))

    returns = {}
    for d in range(count - 1, 0, -1):
        for number, part in enumerate(parts):
            returns[d, number] = pltpu.make_async_remote_copy(
                src_ref=update.at[peer[d], part], dst_ref=update_in.at[me, part], send_sem=send_sem.at[0, d, number],
                recv_sem=recv_sem.at[0, d, number], device_id=(rep, peer[d]), device_id_type=MESH)
            returns[d, number].start()

    scale = learn_rate * 0.2 * math.sqrt(rows * count)
    passed = {}
    for d, number, part in every:
        loads[d, number].wait()
        if d:
            returns[d, number].wait_recv()
            change = update_in[peer[d], part]
        else:
            change = update[me, part]
        stepped[peer[d], part] = (
            w_v[peer[d], part].astype(F32) * (1.0 - learn_rate * decay_rate) - scale * change.astype(F32)
        ).astype(BF16)
        if masks is not None:
            passed[d, number] = pltpu.make_async_remote_copy(
                src_ref=stepped.at[peer[d], part], dst_ref=received.at[peer[d], part],
                send_sem=send_sem.at[1, d, number], recv_sem=recv_sem.at[1, d, number],
                device_id=(mate, me), device_id_type=MESH)
            passed[d, number].start()
    if masks is None:
        averaged[...] = stepped[...]
    else:
        for d, number, part in every:
            passed[d, number].wait_recv()
            averaged[peer[d], part] = (
                (stepped[peer[d], part].astype(F32) + received[peer[d], part].astype(F32)) * 0.5
            ).astype(BF16)
    for copy in list(returns.values()) + list(passed.values()):
        copy.wait_send()


def params(number, limit):
    return pltpu.CompilerParams(collective_id=number, has_side_effects=True, vmem_limit_bytes=limit * 1024 * 1024)


def orthogonalized(number, momentum, gradient, partner):
    count = lax.axis_size("fsdp")
    _, _, rows, cols = momentum.shape
    tile = pltpu.VMEM((count, rows, cols), BF16)
    square = (cols, cols)
    return pl.pallas_call(
        functools.partial(gather_and_iterate, count),
        out_shape=[jax.ShapeDtypeStruct((count, rows, cols), BF16), jax.ShapeDtypeStruct((1,), jnp.int32)],
        in_specs=[pl.BlockSpec(memory_space=pltpu.HBM)] * 3,
        out_specs=[pl.BlockSpec(memory_space=pltpu.VMEM), pl.BlockSpec(memory_space=pltpu.SMEM)],
        scratch_shapes=[tile] * 4
        + [pltpu.VMEM((cols, rows * count), BF16), pltpu.VMEM(square, F32)]
        + [pltpu.VMEM(square, BF16)] * 2
        + [pltpu.SMEM(partner.shape, jnp.int32), pltpu.SemaphoreType.DMA]
        + [pltpu.SemaphoreType.DMA((2, count, PIECES))]
        + [pltpu.SemaphoreType.DMA((count, PIECES))] * 2,
        compiler_params=params(number, 60),
    )(momentum[0], gradient[0], partner)


def finished(masks, number, update, weights):
    count = lax.axis_size("fsdp")
    tile = pltpu.VMEM(weights.shape[1:], BF16)
    return pl.pallas_call(
        functools.partial(return_and_average, count, masks),
        out_shape=jax.ShapeDtypeStruct(weights.shape[1:], BF16),
        in_specs=[pl.BlockSpec(memory_space=pltpu.VMEM), pl.BlockSpec(memory_space=pltpu.HBM)],
        out_specs=pl.BlockSpec(memory_space=pltpu.VMEM),
        scratch_shapes=[tile] * 4
        + [pltpu.SemaphoreType.DMA((count, 1))]
        + [pltpu.SemaphoreType.DMA((2, count, 1))] * 2,
        compiler_params=params(number, 24),
    )(update, weights[0])


def averaged_by_permutes(stepped, partner):
    rep_count = lax.axis_size("rep")
    own_index = lax.axis_index("rep")
    differ = jnp.bitwise_xor(partner[own_index], own_index)
    received = jnp.zeros_like(stepped)
    for bit_number in range(rep_count.bit_length() - 1):
        other = swapped(stepped, "rep", bit_number)
        received = jnp.where(differ == 1 << bit_number, other, received)
    return ((stepped.astype(F32) + received.astype(F32)) * 0.5).astype(BF16)


def local(weights, momentum, gradient, partner):
    update, case = orthogonalized(0, momentum, gradient, partner)
    if lax.axis_size("rep") != 8:
        return averaged_by_permutes(finished(None, 1, update, weights)[None], partner)
    branches = [
        functools.partial(finished, (first, last), 1 + 3 * row + column)
        for row, first in enumerate((1, 2, 4))
        for column, last in enumerate((1, 2, 4))
    ]
    return lax.switch(case[0], branches, update, weights)[None]


def solution(mesh):
    spec = P("rep", None, "fsdp", None)
    return jax.shard_map(local, mesh=mesh, in_specs=(spec, spec, spec, P()), out_specs=spec, check_vma=False)
```
